128 devices in a mesh: row: 16 (over z_lo, x, core), col: 8 (over y, z_hi).
Axes of the slice: x: 4, y: 4, z: 4 (z_hi: 2, z_lo: 2; z = z_hi * 2 + z_lo), core: 2. Of those that a mesh axis runs over, the one named last changes fastest.
Arguments:
- matrix: bfloat16 [9216, 9216], P('row', 'col'), may hold values from -8 to 8
- inverse_factor: bfloat16 [9216, 9216], P('row', 'col'), may hold values from -2 to 2, as said below
Outputs:
- reduced: float32 [9216, 9216], P('col', 'row')
The draws below stay inside these ranges and needn't reach their ends.
Inputs may be any that keep to these rules, and one draw needn't show every extreme that they name: inverse_factor is zero above its diagonal; its diagonal lies in 0.4 to 1.6.
All inputs are finite; a program needn't handle non-finite values.
Results may differ from the reference program's by a relative error of at most 0.0029.
Values may be sent and summed in bfloat16 or wider, within the bound.
A program may use at most 128 MiB of HBM per device.

```python
import math
import jax
import jax.numpy as jnp
from jax import lax

ORDER = 9216


def draw_matrix(key, part):
    key = jax.random.fold_in(key, 11)
    first_key = jax.random.fold_in(key, 0)
    base = jnp.clip(jax.random.normal(first_key, (ORDER, ORDER), jnp.float32), -4.0, 4.0)
    symmetric = (base + base.T) * 0.7071
    return symmetric.astype(jnp.bfloat16)


def draw_inverse_factor(key, part):
    key = jax.random.fold_in(key, 23)
    first_key, second_key = jax.random.split(key)
    row_index = lax.broadcasted_iota(jnp.int32, (ORDER, ORDER), 0)
    col_index = lax.broadcasted_iota(jnp.int32, (ORDER, ORDER), 1)
    below = jnp.clip(jax.random.normal(first_key, (ORDER, ORDER), jnp.float32), -4.0, 4.0) / math.sqrt(ORDER)
    diagonal = jax.random.uniform(second_key, (ORDER,), jnp.float32, 0.5, 1.5)
    on_diagonal = jnp.where(row_index == col_index, diagonal[:, None], 0.0)
    factor = jnp.where(row_index > col_index, below, on_diagonal)
    return factor.astype(jnp.bfloat16)


def setup_inputs(seed: int = 0) -> dict:
    streams_of = jax.random.split(jax.random.key(seed), 3)
    return {
        "matrix": draw_matrix(jax.random.fold_in(streams_of[2], 71), 0),
        "inverse_factor": draw_inverse_factor(jax.random.fold_in(streams_of[2], 71), 0),
    }


def reference(matrix, inverse_factor):
    left = jnp.dot(inverse_factor, matrix, preferred_element_type=jnp.float32).astype(jnp.bfloat16)
    return jnp.dot(left, inverse_factor.T, preferred_element_type=jnp.float32)
```

```python
import jax
import jax.numpy as jnp
from jax import lax
from jax.experimental import pallas as pl
from jax.experimental.pallas import tpu as pltpu
from jax.sharding import PartitionSpec as P

BF16, F32 = jnp.bfloat16, jnp.float32


def kernel(a_ref, l_ref, o_ref, abuf, lbuf, fbuf, acc, lbf, ssem, rsem, csem):
    rows, cols = a_ref.shape
    half = rows // 2
    row, c = lax.axis_index("row"), lax.axis_index("col")
    h, p = row % 2, row // 2
    x, zl = p % 4, p // 4
    y, zh = c // 2, c % 2

    def chip(px, pz):
        return (pz % 2) * 4 + px % 4

    def on_row(pp):
        return (pp * 2 + h, c)

    xp, xm = on_row(chip(x + 1, zl)), on_row(chip(x + 3, zl))
    zp = on_row(chip(x, zl + 1))
    sib = (p * 2 + 1 - h, c)
    yp = (row, ((y + 1) % 4) * 2 + zh)
    ym = (row, ((y + 3) % 4) * 2 + zh)
    hp = (row, y * 2 + 1 - zh)

    t_chip = chip(x + y + 2 * h, zh)
    t_dst = (t_chip * 2 + h, p)

    def kap(px, pz, hh):
        return 2 * ((px - c % 4 - 2 * hh + 8) % 4) + pz % 2

    t_src = (c * 2 + h, kap(x, zl, h))
    t_self = (p == c) & (t_chip == p)

    send_n = [0]
    recv_ids = {}
    sends = []

    def rid(role):
        return recv_ids.setdefault(role, len(recv_ids))

    def send(src, dst, role, device):
        i = send_n[0]
        send_n[0] += 1
        cp = pltpu.make_async_remote_copy(
            src, dst, ssem.at[i], rsem.at[rid(role)], device_id=device,
            device_id_type=pl.DeviceIdType.MESH)
        cp.start()
        sends.append(cp)

    def wait(ref, role):
        pltpu.make_async_remote_copy(
            ref, ref, ssem.at[0], rsem.at[rid(role)], device_id=xp,
            device_id_type=pl.DeviceIdType.MESH).wait_recv()

    barrier = pltpu.get_barrier_semaphore()
    for device in (xp, xm, zp, sib, yp, ym, hp):
        pl.semaphore_signal(barrier, inc=1, device_id=device, device_id_type=pl.DeviceIdType.MESH)

    @pl.when(jnp.logical_not(t_self))
    def _():
        for device in (t_dst, t_src):
            pl.semaphore_signal(barrier, inc=1, device_id=device, device_id_type=pl.DeviceIdType.MESH)

    pl.semaphore_wait(barrier, jnp.where(t_self, 7, 9))

    def a_at(d, q, hh, lo=0, n=rows):
        start = pl.multiple_of((chip(x + d, zl + q) * 2 + hh) * rows + lo, 16)
        return abuf.at[pl.ds(start, n)]

    def l_at(d, q, lo=0, n=rows):
        return lbuf.at[((y + d) % 4) * 2 + (zh + q) % 2, pl.ds(lo, n)]

    def a_send(src, d, q, lo, n, role, device):
        send(src, a_at(d, q, h, lo, n), role, device)

    own_a = a_at(0, 0, h)
    own_l = l_at(0, 0)
    send(a_ref, own_a, "a30", xp)
    send(l_ref, own_l, "l30", yp)
    send(a_ref, own_a, "a10", xm)
    send(l_ref, own_l, "l10", ym)
    send(a_ref, own_a, "a01", zp)
    send(l_ref, own_l, "l01", hp)
    send(a_ref, own_a, "sa00", sib)
    ca = pltpu.make_async_copy(a_ref, own_a, csem.at[0])
    cl = pltpu.make_async_copy(l_ref, own_l, csem.at[1])
    ca.start()
    cl.start()
    acc[...] = jnp.zeros_like(acc)
    o_ref[...] = jnp.zeros_like(o_ref)

    def got(d, q, part=""):
        lo, n = {"": (0, rows), "t": (0, half), "b": (half, half)}[part]
        return a_at(d, q, h, lo, n), l_at(d, q, lo, n), a_at(d, q, 1 - h, lo, n)

    def arrive(d, q, part=""):
        tag = f"{d}{q}{part}"
        ra, rl, _ = got(d, q, part)
        wait(ra, "a" + tag)
        wait(rl, "l" + tag)
        send(ra, ra, "sa" + tag, sib)

    def forward(d, q, part, role, which):
        ra, rl, _ = got(d, q, part)
        send(ra, ra, "a" + role, xp if which else xm)
        send(rl, rl, "l" + role, yp if which else ym)

    def from_sib(d, q, part=""):
        wait(got(d, q, part)[2], f"sa{d}{q}{part}")

    def stage_of(d, q):
        near = jnp.where(d == 0, 1, jnp.where(d == 2, 2, 1))
        far = jnp.where(d == 0, 1, jnp.where(d == 2, 4, 3))
        return jnp.where(q == 0, near, far)

    tile = 384

    def left_stage(stage):
        def step(k, carry):
            sa = stage_of((k % 4 - x + 4) % 4, (k // 4 + zl) % 2)
            sl = stage_of((k // 2 - y + 4) % 4, (k % 2 + zh) % 2)

            @pl.when((jnp.maximum(sa, sl) == stage) & (k <= p))
            def _():
                krow = pl.multiple_of(k * cols, cols)

                def part(j, carry):
                    at = pl.ds(pl.multiple_of(j * tile, tile), tile)
                    acc[:, at] += jnp.dot(
                        lbuf[k], abuf[pl.ds(krow, cols), at], preferred_element_type=F32)
                    return carry

                lax.fori_loop(0, cols // tile, part, 0)
            return carry

        lax.fori_loop(0, 8, step, 0)

    arrive(3, 0)
    forward(3, 0, "t", "20t", True)
    arrive(1, 0)
    forward(1, 0, "b", "20b", False)
    arrive(0, 1)
    forward(0, 1, "", "31", True)
    forward(0, 1, "", "11", False)
    ca.wait()
    cl.wait()
    from_sib(0, 0)
    from_sib(3, 0)
    from_sib(1, 0)
    from_sib(0, 1)
    left_stage(1)
    arrive(2, 0, "t")
    arrive(2, 0, "b")
    from_sib(2, 0, "t")
    from_sib(2, 0, "b")
    left_stage(2)
    arrive(3, 1)
    forward(3, 1, "t", "21t", True)
    arrive(1, 1)
    forward(1, 1, "b", "21b", False)
    from_sib(3, 1)
    from_sib(1, 1)
    left_stage(3)
    arrive(2, 1, "t")
    arrive(2, 1, "b")
    from_sib(2, 1, "t")
    from_sib(2, 1, "b")
    left_stage(4)

    parts = ((0, "t"), (half, "b"))
    lbf[...] = acc[...].astype(BF16)

    def f_at(d, q, hh, lo):
        start = pl.multiple_of(hh * rows + lo, 16)
        return fbuf.at[kap(x + d, zl + q, hh), pl.ds(start, half)]

    turn = []
    for lo, tag in parts:
        src = lbf.at[pl.ds(lo, half)]
        dst = fbuf.at[c, pl.ds(pl.multiple_of(h * rows + lo, 16), half)]
        i = send_n[0]
        send_n[0] += 1
        rsem_at = rsem.at[rid("f00" + tag)]
        cp = pltpu.make_async_remote_copy(
            src, dst, ssem.at[i], rsem_at, device_id=t_dst,
            device_id_type=pl.DeviceIdType.MESH)
        turn.append(cp)

        @pl.when(jnp.logical_not(t_self))
        def _():
            cp.start()

        @pl.when(t_self)
        def _():
            pltpu.make_async_copy(src, dst, rsem_at).start()

    def f_send(d, q, lo, role, device):
        ref = f_at(d, q, h, lo)
        send(ref, ref, role, device)

    def f_arrive(d, q, lo, tag):
        wait(f_at(d, q, h, lo), f"f{d}{q}{tag}")

    def f_sib(d, q, lo, tag):
        f_send(d, q, lo, f"sf{d}{q}{tag}", sib)

    for lo, tag in parts:
        f_arrive(0, 0, lo, tag)
        f_send(0, 0, lo, "f30" + tag, xp)
        f_send(0, 0, lo, "f10" + tag, xm)
        f_send(0, 0, lo, "f01" + tag, zp)
        f_sib(0, 0, lo, tag)

    def out_unit(d, q, hh):
        k = kap(x + d, zl + q, hh)

        @pl.when(k <= p)
        def _():
            step = rows // 3

            def part(j, carry):
                at = pl.ds(pl.multiple_of(hh * rows + j * step, 64), step)
                o_ref[at, :] += lax.dot_general(
                    fbuf[k, at, :], lbuf[k], (((1,), (1,)), ((), ())),
                    preferred_element_type=F32)
                return carry

            lax.fori_loop(0, 3, part, 0)

    def out_stage(blocks):
        for d, q in blocks:
            for lo, tag in parts:
                wait(f_at(d, q, 1 - h, lo), f"sf{d}{q}{tag}")
        first = blocks[0]

        def step(i, carry):
            j, hh = i // 2, i % 2
            d, q = first
            for n, (dd, qq) in enumerate(blocks[1:], 1):
                d = jnp.where(j == n, dd, d)
                q = jnp.where(j == n, qq, q)
            out_unit(d, q, hh)
            return carry

        lax.fori_loop(0, 2 * len(blocks), step, 0)

    out_stage([(0, 0)])
    (top, _), (bot, _) = parts
    f_arrive(3, 0, top, "t")
    f_send(3, 0, top, "f20t", xp)
    f_sib(3, 0, top, "t")
    f_arrive(1, 0, top, "t")
    f_sib(1, 0, top, "t")
    f_arrive(0, 1, top, "t")
    f_send(0, 1, top, "f31t", xp)
    f_send(0, 1, top, "f11t", xm)
    f_sib(0, 1, top, "t")
    f_arrive(1, 0, bot, "b")
    f_send(1, 0, bot, "f20b", xm)
    f_sib(1, 0, bot, "b")
    f_arrive(3, 0, bot, "b")
    f_sib(3, 0, bot, "b")
    f_arrive(0, 1, bot, "b")
    f_send(0, 1, bot, "f31b", xp)
    f_send(0, 1, bot, "f11b", xm)
    f_sib(0, 1, bot, "b")
    out_stage([(3, 0), (1, 0), (0, 1)])
    for lo, tag in parts:
        f_arrive(2, 0, lo, tag)
        f_send(2, 0, lo, "f21" + tag, zp)
        f_sib(2, 0, lo, tag)
    out_stage([(2, 0)])
    for lo, tag in parts:
        for d in (3, 1):
            f_arrive(d, 1, lo, tag)
            f_sib(d, 1, lo, tag)
    out_stage([(3, 1), (1, 1)])
    for lo, tag in parts:
        f_arrive(2, 1, lo, tag)
        f_sib(2, 1, lo, tag)
    out_stage([(2, 1)])

    for cp in sends:
        cp.wait_send()

    @pl.when(jnp.logical_not(t_self))
    def _():
        for cp in turn:
            cp.wait_send()


SENDS, RECVS = 96, 96


def body(matrix, inverse_factor):
    rows, cols = matrix.shape
    order = 16 * rows
    return pl.pallas_call(
        kernel,
        out_shape=jax.ShapeDtypeStruct((cols, rows), F32),
        in_specs=[pl.BlockSpec(memory_space=pl.ANY)] * 2,
        out_specs=pl.BlockSpec(memory_space=pltpu.VMEM),
        scratch_shapes=[
            pltpu.VMEM((order, cols), BF16),
            pltpu.VMEM((8, rows, cols), BF16),
            pltpu.VMEM((8, cols, cols), BF16),
            pltpu.VMEM((rows, cols), F32),
            pltpu.VMEM((rows, cols), BF16),
            pltpu.SemaphoreType.DMA((SENDS,)),
            pltpu.SemaphoreType.DMA((RECVS,)),
            pltpu.SemaphoreType.DMA((2,)),
        ],
        compiler_params=pltpu.CompilerParams(
            collective_id=0, has_side_effects=True, vmem_limit_bytes=63 * 1024 * 1024),
        cost_estimate=pl.CostEstimate(
            flops=4 * rows * cols * order, bytes_accessed=8 * rows * cols, transcendentals=0),
    )(matrix, inverse_factor)


def solution(mesh):
    in_specs = (P("row", "col"), P("row", "col"))
    return jax.shard_map(body, mesh=mesh, in_specs=in_specs, out_specs=P("col", "row"), check_vma=False)
```

```python
import jax
import jax.numpy as jnp
from jax import lax
from jax.experimental import pallas as pl
from jax.experimental.pallas import tpu as pltpu
from jax.sharding import PartitionSpec as P

BF16, F32 = jnp.bfloat16, jnp.float32


def kernel(a_ref, l_ref, o_ref, abuf, lbuf, fbuf, acc, lbf, ssem, rsem, csem):
    rows, cols = a_ref.shape
    row, c = lax.axis_index("row"), lax.axis_index("col")
    h, p = row % 2, row // 2
    x, zl = p % 4, p // 4
    y, zh = c // 2, c % 2

    def chip(px, pz):
        return (pz % 2) * 4 + px % 4

    def on_row(pp):
        return (pp * 2 + h, c)

    xp, xm = on_row(chip(x + 1, zl)), on_row(chip(x + 3, zl))
    zp = on_row(chip(x, zl + 1))
    sib = (p * 2 + 1 - h, c)
    yp = (row, ((y + 1) % 4) * 2 + zh)
    ym = (row, ((y + 3) % 4) * 2 + zh)
    hp = (row, y * 2 + 1 - zh)

    t_chip = chip(x + y + 2 * h, zh)
    t_dst = (t_chip * 2 + h, p)

    def kap(px, pz, hh):
        return 2 * ((px - c % 4 - 2 * hh + 8) % 4) + pz % 2

    t_src = (c * 2 + h, kap(x, zl, h))
    t_self = (p == c) & (t_chip == p)

    half = rows // 2
    quarter = half // 2
    send_n = [0]
    recv_ids = {}
    sends = []

    def when(cond, f):
        if cond is None:
            f()
        else:
            pl.when(cond)(f)

    def rid(role):
        return recv_ids.setdefault(role, len(recv_ids))

    def send(src, dst, role, device, cond=None):
        i = send_n[0]
        send_n[0] += 1
        cp = pltpu.make_async_remote_copy(
            src, dst, ssem.at[i], rsem.at[rid(role)], device_id=device,
            device_id_type=pl.DeviceIdType.MESH)
        when(cond, cp.start)
        sends.append((cond, cp))

    def drain():
        for cond, cp in sends:
            when(cond, cp.wait_send)
        sends.clear()

    def wait(ref, role, cond=None):
        cp = pltpu.make_async_remote_copy(
            ref, ref, ssem.at[0], rsem.at[rid(role)], device_id=xp,
            device_id_type=pl.DeviceIdType.MESH)
        when(cond, cp.wait_recv)

    barrier = pltpu.get_barrier_semaphore()
    for device in (xp, xm, zp, sib, yp, ym, hp):
        pl.semaphore_signal(barrier, inc=1, device_id=device, device_id_type=pl.DeviceIdType.MESH)

    @pl.when(jnp.logical_not(t_self))
    def _():
        for device in (t_dst, t_src):
            pl.semaphore_signal(barrier, inc=1, device_id=device, device_id_type=pl.DeviceIdType.MESH)

    pl.semaphore_wait(barrier, jnp.where(t_self, 7, 9))

    pieces = {"": (0, rows), "t": (0, half), "b": (half, half),
              "t0": (0, quarter), "t1": (quarter, quarter),
              "b0": (half, quarter), "b1": (half + quarter, quarter)}
    upper, lower = zl == 1, zl == 0

    def need(d):
        return upper | ((y + d) % 4 <= 1)

    def a_at(d, q, hh, piece):
        lo, n = pieces[piece]
        start = pl.multiple_of((chip(x + d, zl + q) * 2 + hh) * rows + lo, 16)
        return abuf.at[pl.ds(start, n)]

    def l_at(d, q, piece):
        lo, n = pieces[piece]
        return lbuf.at[((y + d) % 4) * 2 + (zh + q) % 2, pl.ds(lo, n)]

    def own(ref, piece):
        lo, n = pieces[piece]
        return ref.at[pl.ds(lo, n)]

    def cond_a(q):
        return upper if q else None

    def a_get(d, q, piece):
        ref = a_at(d, q, h, piece)
        wait(ref, f"a{d}{q}{piece}", cond_a(q))
        send(ref, ref, f"sa{d}{q}{piece}", sib, cond_a(q))

    def a_fwd(d, q, piece, to, device, cond):
        ref = a_at(d, q, h, piece)
        send(ref, ref, f"a{to}{piece}", device, cond)

    def a_sib(d, q, *names):
        for piece in names:
            wait(a_at(d, q, 1 - h, piece), f"sa{d}{q}{piece}", cond_a(q))

    def l_get(d, q, piece):
        wait(l_at(d, q, piece), f"l{d}{q}{piece}", need(d))

    def l_fwd(d, q, piece, to, device):
        ref = l_at(d, q, piece)
        send(ref, ref, f"l{to}{piece}", device, need(d))

    tile = 384

    def left_stage(stage, piece):
        lo, n = pieces[piece]
        at_rows = pl.ds(lo, n)
        l_far = (3, 4) if piece == "t" else (5, 5)

        def stage_of(d, q, odd, opposite):
            near = jnp.where(d == 2, 2, 1)
            far = jnp.where(d == 0, 3, jnp.where(d == 2, opposite, odd))
            return jnp.maximum(jnp.where(q == 0, near, far), 2)

        def step(k, carry):
            sa = stage_of((k % 4 - x + 4) % 4, (k // 4 + zl) % 2, 4, 5)
            sl = stage_of((k // 2 - y + 4) % 4, (k % 2 + zh) % 2, *l_far)

            @pl.when((jnp.maximum(sa, sl) == stage) & (k <= p))
            def _():
                krow = pl.multiple_of(k * cols, cols)

                def part(j, carry):
                    at = pl.ds(pl.multiple_of(j * tile, tile), tile)
                    acc[at_rows, at] += jnp.dot(
                        lbuf[k, at_rows], abuf[pl.ds(krow, cols), at],
                        preferred_element_type=F32)
                    return carry

                lax.fori_loop(0, cols // tile, part, 0)
            return carry

        lax.fori_loop(0, 8, step, 0)

    for piece in "tb":
        a_own, l_own = own(a_ref, piece), own(l_ref, piece)
        send(a_own, a_at(0, 0, h, piece), "a30" + piece, xp)
        send(l_own, l_at(0, 0, piece), "l30" + piece, yp, need(0))
        send(a_own, a_at(0, 0, h, piece), "a10" + piece, xm)
        send(l_own, l_at(0, 0, piece), "l10" + piece, ym, need(0))
        if piece == "t":
            first = len(sends)
            send(a_own, a_at(0, 0, h, piece), "a01" + piece, zp, lower)
            send(l_own, l_at(0, 0, piece), "l01" + piece, hp, need(0))
    send(a_ref, a_at(0, 0, h, ""), "sa00", sib)
    ca = pltpu.make_async_copy(a_ref, a_at(0, 0, h, ""), csem.at[0])
    cl = pltpu.make_async_copy(l_ref, l_at(0, 0, ""), csem.at[1])
    ca.start()
    cl.start()
    acc[...] = jnp.zeros_like(acc)
    o_ref[...] = jnp.zeros_like(o_ref)
    ca.wait()
    cl.wait()

    l_get(3, 0, "t")
    l_fwd(3, 0, "t0", "20", yp)
    l_get(1, 0, "t")
    l_fwd(1, 0, "t1", "20", ym)
    a_get(3, 0, "t")
    a_fwd(3, 0, "t", "20", xp, None)
    a_get(1, 0, "t")
    for cond, cp in sends[first:first + 2]:
        when(cond, cp.wait_send)
    del sends[first:first + 2]
    send(own(a_ref, "b"), a_at(0, 0, h, "b"), "a01b", zp, lower)
    send(own(l_ref, "b"), l_at(0, 0, "b"), "l01b", hp, need(0))
    a_get(3, 0, "b")
    a_get(1, 0, "b")
    a_fwd(1, 0, "b", "20", xm, None)
    l_get(0, 1, "t")
    l_fwd(0, 1, "t", "31", yp)
    l_fwd(0, 1, "t", "11", ym)
    a_get(0, 1, "t")
    a_fwd(0, 1, "t", "31", xp, upper)
    a_fwd(0, 1, "t", "11", xm, upper)
    l_get(3, 0, "b")
    l_fwd(3, 0, "b0", "20", yp)
    l_get(1, 0, "b")
    l_fwd(1, 0, "b1", "20", ym)

    a_get(2, 0, "t")
    a_fwd(2, 0, "t", "21", zp, lower)
    a_get(2, 0, "b")
    for piece in ("t0", "t1", "b0", "b1"):
        l_get(2, 0, piece)
    a_sib(0, 0, "")
    a_sib(3, 0, "t", "b")
    a_sib(1, 0, "t", "b")
    a_sib(2, 0, "t", "b")
    left_stage(2, "t")
    left_stage(2, "b")

    l_get(0, 1, "b")
    l_fwd(0, 1, "b", "31", yp)
    l_fwd(0, 1, "b", "11", ym)
    a_get(0, 1, "b")
    a_fwd(0, 1, "b", "31", xp, upper)
    a_fwd(0, 1, "b", "11", xm, upper)
    l_get(3, 1, "t")
    l_fwd(3, 1, "t0", "21", yp)
    l_get(1, 1, "t")
    l_fwd(1, 1, "t1", "21", ym)
    a_sib(0, 1, "t", "b")
    left_stage(3, "t")
    left_stage(3, "b")

    a_get(3, 1, "t")
    a_get(1, 1, "t")
    a_get(3, 1, "b")
    a_fwd(3, 1, "b0", "21", xp, upper)
    a_get(1, 1, "b")
    a_fwd(1, 1, "b1", "21", xm, upper)
    l_get(2, 1, "t0")
    l_get(2, 1, "t1")
    a_sib(3, 1, "t", "b")
    a_sib(1, 1, "t", "b")
    left_stage(4, "t")
    left_stage(4, "b")
    l_get(3, 1, "b")
    l_fwd(3, 1, "b0", "21", yp)
    l_get(1, 1, "b")
    l_fwd(1, 1, "b1", "21", ym)
    a_get(2, 1, "t")
    a_get(2, 1, "b0")
    a_get(2, 1, "b1")
    a_sib(2, 1, "t", "b0", "b1")

    def f_at(d, q, hh, piece):
        lo, n = pieces[piece]
        start = pl.multiple_of(hh * rows + lo, 16)
        return fbuf.at[kap(x + d, zl + q, hh), pl.ds(start, n)]

    turn = []

    def finish(piece):
        left_stage(5, piece)
        lo, n = pieces[piece]
        lbf[pl.ds(lo, n)] = acc[pl.ds(lo, n)].astype(BF16)
        src = lbf.at[pl.ds(lo, n)]
        dst = fbuf.at[c, pl.ds(pl.multiple_of(h * rows + lo, 16), n)]
        i = send_n[0]
        send_n[0] += 1
        landed = rsem.at[rid("f00" + piece)]
        cp = pltpu.make_async_remote_copy(
            src, dst, ssem.at[i], landed, device_id=t_dst,
            device_id_type=pl.DeviceIdType.MESH)
        when(jnp.logical_not(t_self), cp.start)
        when(t_self, lambda: pltpu.make_async_copy(src, dst, landed).start())
        sends.append((jnp.logical_not(t_self), cp))

    finish("t")
    l_get(2, 1, "b0")
    l_get(2, 1, "b1")
    finish("b")

    def f_get(d, q, piece):
        ref = f_at(d, q, h, piece)
        wait(ref, f"f{d}{q}{piece}")
        send(ref, ref, f"sf{d}{q}{piece}", sib)

    def f_fwd(d, q, piece, to, device):
        ref = f_at(d, q, h, piece)
        send(ref, ref, f"f{to}{piece}", device)

    def out_stage(blocks):
        for d, q, piece in blocks:
            wait(f_at(d, q, 1 - h, piece), f"sf{d}{q}{piece}")

        def pick(j, values):
            v = values[0]
            for n, value in enumerate(values[1:], 1):
                v = jnp.where(j == n, value, v)
            return v

        def step(i, carry):
            j, hh = i // 2, i % 2
            d, q = pick(j, [b[0] for b in blocks]), pick(j, [b[1] for b in blocks])
            lo = pick(j, [pieces[b[2]][0] for b in blocks])
            k = kap(x + d, zl + q, hh)

            @pl.when(k <= p)
            def _():
                at = pl.ds(pl.multiple_of(hh * rows + lo, half), half)
                o_ref[at, :] += lax.dot_general(
                    fbuf[k, at, :], lbuf[k], (((1,), (1,)), ((), ())),
                    preferred_element_type=F32)
            return carry

        lax.fori_loop(0, 2 * len(blocks), step, 0)

    for piece in "tb":
        f_get(0, 0, piece)
        f_fwd(0, 0, piece, "30", xp)
        f_fwd(0, 0, piece, "10", xm)
        f_fwd(0, 0, piece, "01", zp)
    f_get(3, 0, "t")
    f_fwd(3, 0, "t", "20", xp)
    f_get(1, 0, "t")
    f_get(0, 1, "t")
    f_fwd(0, 1, "t", "31", xp)
    f_fwd(0, 1, "t", "11", xm)
    f_get(1, 0, "b")
    f_fwd(1, 0, "b", "20", xm)
    f_get(3, 0, "b")
    f_get(0, 1, "b")
    f_fwd(0, 1, "b", "31", xp)
    f_fwd(0, 1, "b", "11", xm)
    out_stage([(0, 0, "t"), (0, 0, "b")])
    f_get(2, 0, "t")
    f_fwd(2, 0, "t", "21", zp)
    f_get(2, 0, "b")
    f_fwd(2, 0, "b", "21", zp)
    out_stage([(3, 0, "t"), (1, 0, "t"), (0, 1, "t"), (3, 0, "b"), (1, 0, "b"), (0, 1, "b")])
    out_stage([(2, 0, "t"), (2, 0, "b")])
    f_get(3, 1, "t")
    f_get(1, 1, "t")
    f_get(2, 1, "t")
    out_stage([(3, 1, "t"), (1, 1, "t"), (2, 1, "t")])
    f_get(2, 1, "b")
    f_get(3, 1, "b")
    f_get(1, 1, "b")
    out_stage([(2, 1, "b"), (3, 1, "b"), (1, 1, "b")])
    drain()


SENDS, RECVS = 160, 160


def body(matrix, inverse_factor):
    rows, cols = matrix.shape
    order = 16 * rows
    return pl.pallas_call(
        kernel,
        out_shape=jax.ShapeDtypeStruct((cols, rows), F32),
        in_specs=[pl.BlockSpec(memory_space=pl.ANY)] * 2,
        out_specs=pl.BlockSpec(memory_space=pltpu.VMEM),
        scratch_shapes=[
            pltpu.VMEM((order, cols), BF16),
            pltpu.VMEM((8, rows, cols), BF16),
            pltpu.VMEM((8, cols, cols), BF16),
            pltpu.VMEM((rows, cols), F32),
            pltpu.VMEM((rows, cols), BF16),
            pltpu.SemaphoreType.DMA((SENDS,)),
            pltpu.SemaphoreType.DMA((RECVS,)),
            pltpu.SemaphoreType.DMA((2,)),
        ],
        compiler_params=pltpu.CompilerParams(
            collective_id=0, has_side_effects=True, vmem_limit_bytes=63 * 1024 * 1024),
        cost_estimate=pl.CostEstimate(
            flops=4 * rows * cols * order, bytes_accessed=8 * rows * cols, transcendentals=0),
    )(matrix, inverse_factor)


def solution(mesh):
    in_specs = (P("row", "col"), P("row", "col"))
    return jax.shard_map(body, mesh=mesh, in_specs=in_specs, out_specs=P("col", "row"), check_vma=False)
```

```python
import jax
import jax.numpy as jnp
from jax import lax
from jax.experimental import pallas as pl
from jax.experimental.pallas import tpu as pltpu
from jax.sharding import PartitionSpec as P

BF16, F32 = jnp.bfloat16, jnp.float32


def kernel(a_ref, l_ref, o_ref, abuf, lbuf, fbuf, acc, lbf, ssem, rsem, csem):
    rows, cols = a_ref.shape
    row, c = lax.axis_index("row"), lax.axis_index("col")
    h, p = row % 2, row // 2
    x, zl = p % 4, p // 4
    y, zh = c // 2, c % 2

    def chip(px, pz):
        return (pz % 2) * 4 + px % 4

    def on_row(pp):
        return (pp * 2 + h, c)

    xp, xm = on_row(chip(x + 1, zl)), on_row(chip(x + 3, zl))
    zp = on_row(chip(x, zl + 1))
    sib = (p * 2 + 1 - h, c)
    yp = (row, ((y + 1) % 4) * 2 + zh)
    ym = (row, ((y + 3) % 4) * 2 + zh)
    hp = (row, y * 2 + 1 - zh)

    t_chip = chip(x + y + 2 * h, zh)
    t_dst = (t_chip * 2 + h, p)

    def kap(px, pz, hh):
        return 2 * ((px - c % 4 - 2 * hh + 8) % 4) + pz % 2

    t_src = (c * 2 + h, kap(x, zl, h))
    t_self = (p == c) & (t_chip == p)

    half = rows // 2
    send_n = [0]
    recv_ids = {}
    sends = []

    def when(cond, f):
        if cond is None:
            f()
        else:
            pl.when(cond)(f)

    def rid(role):
        return recv_ids.setdefault(role, len(recv_ids))

    def send(src, dst, role, device, cond=None):
        i = send_n[0]
        send_n[0] += 1
        cp = pltpu.make_async_remote_copy(
            src, dst, ssem.at[i], rsem.at[rid(role)], device_id=device,
            device_id_type=pl.DeviceIdType.MESH)
        when(cond, cp.start)
        sends.append((cond, cp))

    def drain():
        for cond, cp in sends:
            when(cond, cp.wait_send)
        sends.clear()

    def wait(ref, role, cond=None):
        cp = pltpu.make_async_remote_copy(
            ref, ref, ssem.at[0], rsem.at[rid(role)], device_id=xp,
            device_id_type=pl.DeviceIdType.MESH)
        when(cond, cp.wait_recv)

    barrier = pltpu.get_barrier_semaphore()
    for device in (xp, xm, zp, sib, yp, ym, hp):
        pl.semaphore_signal(barrier, inc=1, device_id=device, device_id_type=pl.DeviceIdType.MESH)

    @pl.when(jnp.logical_not(t_self))
    def _():
        for device in (t_dst, t_src):
            pl.semaphore_signal(barrier, inc=1, device_id=device, device_id_type=pl.DeviceIdType.MESH)

    pl.semaphore_wait(barrier, jnp.where(t_self, 7, 9))

    quarter = half // 2
    row_part = {"": (0, rows), "t": (0, half), "b": (half, half),
                "t0": (0, quarter), "t1": (quarter, quarter),
                "b0": (half, quarter), "b1": (half + quarter, quarter)}
    split = (cols // 256 + 1) * 128
    col_part = {"": (0, cols), "L": (0, split), "R": (split, cols - split)}
    upper, lower = zl == 1, zl == 0

    def cut(ref, start, rp, cp):
        lo, n = row_part[rp]
        at, m = col_part[cp]
        return ref.at[pl.ds(pl.multiple_of(start + lo, 16), n), pl.ds(at, m)]

    def need(d):
        return upper | ((y + d) % 4 <= 1)

    def a_at(d, q, hh, rp, cp):
        return cut(abuf, (chip(x + d, zl + q) * 2 + hh) * rows, rp, cp)

    def l_at(d, q, rp):
        return cut(lbuf.at[((y + d) % 4) * 2 + (zh + q) % 2], 0, rp, "")

    def cond_a(q):
        return upper if q else None

    def a_get(d, q, rp, cp):
        ref = a_at(d, q, h, rp, cp)
        wait(ref, f"a{d}{q}{rp}{cp}", cond_a(q))
        send(ref, ref, f"sa{d}{q}{rp}{cp}", sib, cond_a(q))

    def a_fwd(d, q, rp, cp, to, device, cond):
        ref = a_at(d, q, h, rp, cp)
        send(ref, ref, f"a{to}{rp}{cp}", device, cond)

    def a_sib(d, q, cp, *names):
        for rp in names:
            wait(a_at(d, q, 1 - h, rp, cp), f"sa{d}{q}{rp}{cp}", cond_a(q))

    def l_get(d, q, rp):
        wait(l_at(d, q, rp), f"l{d}{q}{rp}", need(d))

    def l_fwd(d, q, rp, to, device):
        ref = l_at(d, q, rp)
        send(ref, ref, f"l{to}{rp}", device, need(d))

    def a_own(cp, ways):
        src = cut(a_ref, 0, "", cp)
        for role, device, cond in ways:
            send(src, a_at(0, 0, h, "", cp), f"a{role}{cp}", device, cond)

    def l_own(rp, ways):
        src = cut(l_ref, 0, rp, "")
        for role, device in ways:
            send(src, l_at(0, 0, rp), f"l{role}{rp}", device, need(0))

    def left_stage(stage, rp, cp):
        lo, n = row_part[rp]
        at, m = col_part[cp]
        at_rows, at_cols = pl.ds(lo, n), pl.ds(at, m)

        def stage_of(d, q, first):
            return jnp.where((q == 0) | (d == 0), first, first + 1)

        def step(k, carry):
            sa = stage_of((k % 4 - x + 4) % 4, (k // 4 + zl) % 2, 1 if cp == "L" else 3)
            sl = stage_of((k // 2 - y + 4) % 4, (k % 2 + zh) % 2, 1 if rp == "t" else 3)

            @pl.when((jnp.maximum(sa, sl) == stage) & (k <= p))
            def _():
                krow = pl.multiple_of(k * cols, cols)
                acc[at_rows, at_cols] += jnp.dot(
                    lbuf[k, at_rows], abuf[pl.ds(krow, cols), at_cols],
                    preferred_element_type=F32)

            return carry

        lax.fori_loop(0, 8, step, 0)

    def f_at(d, q, hh, rp, cp):
        return cut(fbuf.at[kap(x + d, zl + q, hh)], hh * rows, rp, cp)

    def finish(rp, cp):
        lo, n = row_part[rp]
        at, m = col_part[cp]
        lbf[pl.ds(lo, n), pl.ds(at, m)] = acc[pl.ds(lo, n), pl.ds(at, m)].astype(BF16)
        src = cut(lbf, 0, rp, cp)
        dst = cut(fbuf.at[c], h * rows, rp, cp)
        i = send_n[0]
        send_n[0] += 1
        landed = rsem.at[rid(f"f00{rp}{cp}")]
        copy = pltpu.make_async_remote_copy(
            src, dst, ssem.at[i], landed, device_id=t_dst,
            device_id_type=pl.DeviceIdType.MESH)
        when(jnp.logical_not(t_self), copy.start)
        when(t_self, lambda: pltpu.make_async_copy(src, dst, landed).start())
        sends.append((jnp.logical_not(t_self), copy))

    def f_fwd(d, q, piece, to, device):
        ref = f_at(d, q, h, *piece)
        send(ref, ref, "f" + to + piece, device)

    def f_get(piece, *roles):
        for d, q in roles:
            ref = f_at(d, q, h, *piece)
            wait(ref, f"f{d}{q}{piece}")
            if (d, q) == (0, 0):
                f_fwd(d, q, piece, "30", xp)
                f_fwd(d, q, piece, "10", xm)
                f_fwd(d, q, piece, "01", zp)
            elif (d, q) == (3, 0) and piece[0] == "t":
                f_fwd(d, q, piece, "20", xp)
            elif (d, q) == (1, 0) and piece[0] == "b":
                f_fwd(d, q, piece, "20", xm)
            elif (d, q) == (0, 1):
                f_fwd(d, q, piece, "31", xp)
                f_fwd(d, q, piece, "11", xm)
            elif (d, q) == (2, 0):
                f_fwd(d, q, piece, "21", zp)
            send(ref, ref, f"sf{d}{q}{piece}", sib)

    def out_stage(cp, *roles):
        for d, q in roles:
            for rp in "tb":
                wait(f_at(d, q, 1 - h, rp, cp), f"sf{d}{q}{rp}{cp}")
        at_cols = pl.ds(*col_part[cp])

        def pick(j, values):
            v = values[0]
            for n, value in enumerate(values[1:], 1):
                v = jnp.where(j == n, value, v)
            return v

        def step(i, carry):
            j, hh = i // 2, i % 2
            d, q = pick(j, [r[0] for r in roles]), pick(j, [r[1] for r in roles])
            k = kap(x + d, zl + q, hh)

            @pl.when(k <= p)
            def _():
                at = pl.ds(pl.multiple_of(hh * rows, rows), rows)
                o_ref[at, :] += lax.dot_general(
                    fbuf[k, at, at_cols], lbuf[k, :, at_cols], (((1,), (1,)), ((), ())),
                    preferred_element_type=F32)
            return carry

        lax.fori_loop(0, 2 * len(roles), step, 0)

    ring = (("30", xp, None), ("10", xm, None))
    a_own("L", ring)
    l_own("t", (("30", yp), ("10", ym)))
    first = len(sends)
    a_own("L", (("01", zp, lower),))
    l_own("t", (("01", hp),))
    send(a_ref, a_at(0, 0, h, "", ""), "sa00", sib)
    ca = pltpu.make_async_copy(a_ref, a_at(0, 0, h, "", ""), csem.at[0])
    cl = pltpu.make_async_copy(l_ref, l_at(0, 0, ""), csem.at[1])
    ca.start()
    cl.start()
    acc[...] = jnp.zeros_like(acc)
    o_ref[...] = jnp.zeros_like(o_ref)
    ca.wait()
    cl.wait()

    l_get(3, 0, "t")
    l_fwd(3, 0, "t0", "20", yp)
    l_get(1, 0, "t")
    l_fwd(1, 0, "t1", "20", ym)
    l_own("b", (("30", yp), ("10", ym)))
    a_get(3, 0, "", "L")
    a_fwd(3, 0, "t", "L", "20", xp, None)
    a_get(1, 0, "", "L")
    a_fwd(1, 0, "b", "L", "20", xm, None)
    a_own("R", ring)
    for cond, copy in sends[first:first + 2]:
        when(cond, copy.wait_send)
    del sends[first:first + 2]
    a_own("R", (("01", zp, lower),))
    l_own("b", (("01", hp),))
    l_get(0, 1, "t")
    l_fwd(0, 1, "t", "31", yp)
    l_fwd(0, 1, "t", "11", ym)
    a_get(0, 1, "", "L")
    a_fwd(0, 1, "", "L", "31", xp, upper)
    a_fwd(0, 1, "", "L", "11", xm, upper)
    a_get(2, 0, "t", "L")
    a_fwd(2, 0, "t", "L", "21", zp, lower)
    a_get(2, 0, "b", "L")
    l_get(3, 0, "b")
    l_fwd(3, 0, "b0", "20", yp)
    l_get(1, 0, "b")
    l_fwd(1, 0, "b1", "20", ym)
    a_get(3, 0, "", "R")
    a_fwd(3, 0, "t", "R", "20", xp, None)
    a_get(1, 0, "", "R")
    a_fwd(1, 0, "b", "R", "20", xm, None)
    l_get(2, 0, "t0")
    l_get(2, 0, "t1")
    wait(a_at(0, 0, 1 - h, "", ""), "sa00")
    for d in (3, 1):
        a_sib(d, 0, "L", "")
    a_sib(0, 1, "L", "")
    a_sib(2, 0, "L", "t", "b")
    left_stage(1, "t", "L")

    l_get(3, 1, "t")
    l_fwd(3, 1, "t0", "21", yp)
    l_get(1, 1, "t")
    l_fwd(1, 1, "t1", "21", ym)
    a_get(3, 1, "", "L")
    a_fwd(3, 1, "b0", "L", "21", xp, upper)
    a_get(1, 1, "", "L")
    a_fwd(1, 1, "b1", "L", "21", xm, upper)
    l_get(0, 1, "b")
    l_fwd(0, 1, "b", "31", yp)
    l_fwd(0, 1, "b", "11", ym)
    a_get(0, 1, "", "R")
    a_fwd(0, 1, "", "R", "31", xp, upper)
    a_fwd(0, 1, "", "R", "11", xm, upper)
    a_get(2, 0, "t", "R")
    a_fwd(2, 0, "t", "R", "21", zp, lower)
    a_get(2, 0, "b", "R")
    for rp in ("t", "b0", "b1"):
        a_get(2, 1, rp, "L")
    l_get(2, 1, "t0")
    l_get(2, 1, "t1")
    for d in (3, 1):
        a_sib(d, 1, "L", "")
    a_sib(2, 1, "L", "t", "b0", "b1")
    left_stage(2, "t", "L")
    finish("t", "L")

    l_get(2, 0, "b0")
    l_get(2, 0, "b1")
    for d in (3, 1):
        a_sib(d, 0, "R", "")
    a_sib(0, 1, "R", "")
    a_sib(2, 0, "R", "t", "b")
    left_stage(3, "b", "L")
    left_stage(3, "t", "R")
    left_stage(3, "b", "R")

    l_get(3, 1, "b")
    l_fwd(3, 1, "b0", "21", yp)
    l_get(1, 1, "b")
    l_fwd(1, 1, "b1", "21", ym)
    a_get(3, 1, "", "R")
    a_fwd(3, 1, "b0", "R", "21", xp, upper)
    a_get(1, 1, "", "R")
    a_fwd(1, 1, "b1", "R", "21", xm, upper)
    f_get("tL", (0, 0))
    l_get(2, 1, "b0")
    l_get(2, 1, "b1")
    left_stage(4, "b", "L")
    finish("b", "L")
    for rp in ("t", "b0", "b1"):
        a_get(2, 1, rp, "R")
    for d in (3, 1):
        a_sib(d, 1, "R", "")
    a_sib(2, 1, "R", "t", "b0", "b1")
    left_stage(4, "t", "R")
    finish("t", "R")
    f_get("tL", (3, 0), (1, 0), (0, 1))
    left_stage(4, "b", "R")
    finish("b", "R")

    near = ((3, 0), (1, 0), (0, 1))
    far = ((3, 1), (1, 1), (2, 1))
    f_get("tL", (2, 0))
    f_get("bL", (0, 0))
    f_get("tR", (0, 0))
    f_get("bL", *near)
    f_get("bR", (0, 0))
    f_get("tL", *far)
    f_get("tR", *near)
    f_get("bL", (2, 0))
    out_stage("L", (0, 0), *near)
    f_get("bR", *near)
    f_get("tR", (2, 0))
    f_get("bL", *far)
    f_get("bR", (2, 0))
    out_stage("R", (0, 0), *near)
    out_stage("L", (2, 0), *far)
    f_get("tR", *far)
    out_stage("R", (2, 0))
    f_get("bR", *far)
    out_stage("R", *far)
    drain()


SENDS, RECVS = 200, 200


def body(matrix, inverse_factor):
    rows, cols = matrix.shape
    order = 16 * rows
    return pl.pallas_call(
        kernel,
        out_shape=jax.ShapeDtypeStruct((cols, rows), F32),
        in_specs=[pl.BlockSpec(memory_space=pl.ANY)] * 2,
        out_specs=pl.BlockSpec(memory_space=pltpu.VMEM),
        scratch_shapes=[
            pltpu.VMEM((order, cols), BF16),
            pltpu.VMEM((8, rows, cols), BF16),
            pltpu.VMEM((8, cols, cols), BF16),
            pltpu.VMEM((rows, cols), F32),
            pltpu.VMEM((rows, cols), BF16),
            pltpu.SemaphoreType.DMA((SENDS,)),
            pltpu.SemaphoreType.DMA((RECVS,)),
            pltpu.SemaphoreType.DMA((2,)),
        ],
        compiler_params=pltpu.CompilerParams(
            collective_id=0, has_side_effects=True, vmem_limit_bytes=63 * 1024 * 1024),
        cost_estimate=pl.CostEstimate(
            flops=4 * rows * cols * order, bytes_accessed=8 * rows * cols, transcendentals=0),
    )(matrix, inverse_factor)


def solution(mesh):
    in_specs = (P("row", "col"), P("row", "col"))
    return jax.shard_map(body, mesh=mesh, in_specs=in_specs, out_specs=P("col", "row"), check_vma=False)
```

```python
import jax
import jax.numpy as jnp
from jax import lax
from jax.experimental import pallas as pl
from jax.experimental.pallas import tpu as pltpu
from jax.sharding import PartitionSpec as P

BF16, F32 = jnp.bfloat16, jnp.float32


def kernel(a_ref, l_ref, o_ref, abuf, lbuf, fbuf, acc, lbf, ssem, rsem, csem):
    rows, cols = a_ref.shape
    row, c = lax.axis_index("row"), lax.axis_index("col")
    h, p = row % 2, row // 2
    x, zl = p % 4, p // 4
    y, zh = c // 2, c % 2

    def chip(px, pz):
        return (pz % 2) * 4 + px % 4

    def on_row(pp):
        return (pp * 2 + h, c)

    xp, xm = on_row(chip(x + 1, zl)), on_row(chip(x + 3, zl))
    zp = on_row(chip(x, zl + 1))
    sib = (p * 2 + 1 - h, c)
    yp = (row, ((y + 1) % 4) * 2 + zh)
    ym = (row, ((y + 3) % 4) * 2 + zh)
    hp = (row, y * 2 + 1 - zh)

    t_chip = chip(x + y + 2 * h, zh)
    t_dst = (t_chip * 2 + h, p)

    def kap(px, pz, hh):
        return 2 * ((px - c % 4 - 2 * hh + 8) % 4) + pz % 2

    t_src = (c * 2 + h, kap(x, zl, h))
    t_self = (p == c) & (t_chip == p)

    half = rows // 2
    send_n = [0]
    recv_ids = {}
    sends = []

    def when(cond, f):
        if cond is None:
            f()
        else:
            pl.when(cond)(f)

    def rid(role):
        return recv_ids.setdefault(role, len(recv_ids))

    def send(src, dst, role, device, cond=None):
        i = send_n[0]
        send_n[0] += 1
        cp = pltpu.make_async_remote_copy(
            src, dst, ssem.at[i], rsem.at[rid(role)], device_id=device,
            device_id_type=pl.DeviceIdType.MESH)
        when(cond, cp.start)
        sends.append((cond, cp))

    def drain():
        for cond, cp in sends:
            when(cond, cp.wait_send)
        sends.clear()

    def wait(ref, role, cond=None):
        cp = pltpu.make_async_remote_copy(
            ref, ref, ssem.at[0], rsem.at[rid(role)], device_id=xp,
            device_id_type=pl.DeviceIdType.MESH)
        when(cond, cp.wait_recv)

    barrier = pltpu.get_barrier_semaphore()
    for device in (xp, xm, zp, sib, yp, ym, hp):
        pl.semaphore_signal(barrier, inc=1, device_id=device, device_id_type=pl.DeviceIdType.MESH)

    @pl.when(jnp.logical_not(t_self))
    def _():
        for device in (t_dst, t_src):
            pl.semaphore_signal(barrier, inc=1, device_id=device, device_id_type=pl.DeviceIdType.MESH)

    pl.semaphore_wait(barrier, jnp.where(t_self, 7, 9))

    top, split = half, (cols // 256 + 1) * 128

    def halves(name, lo, n):
        return {name: (lo, n), name + "0": (lo, n // 2), name + "1": (lo + n // 2, n // 2)}

    row_part = {"": (0, rows), "u": (0, half), "v": (half, half),
                **halves("t", 0, top), **halves("b", top, rows - top)}
    col_part = {"": (0, cols), "L": (0, split), "R": (split, cols - split)}
    upper, lower = zl == 1, zl == 0

    def cut(ref, start, rp, cp):
        lo, n = row_part[rp]
        at, m = col_part[cp]
        return ref.at[pl.ds(pl.multiple_of(start + lo, 16), n), pl.ds(at, m)]

    def need(d):
        return upper | ((y + d) % 4 <= 1)

    def a_at(d, q, hh, rp, cp):
        return cut(abuf, (chip(x + d, zl + q) * 2 + hh) * rows, rp, cp)

    def l_at(d, q, rp):
        return cut(lbuf.at[((y + d) % 4) * 2 + (zh + q) % 2], 0, rp, "")

    def cond_a(q):
        return upper if q else None

    def a_get(d, q, rp, cp):
        ref = a_at(d, q, h, rp, cp)
        wait(ref, f"a{d}{q}{rp}{cp}", cond_a(q))
        send(ref, ref, f"sa{d}{q}{rp}{cp}", sib, cond_a(q))

    def a_fwd(d, q, rp, cp, to, device, cond):
        ref = a_at(d, q, h, rp, cp)
        send(ref, ref, f"a{to}{rp}{cp}", device, cond)

    def a_sib(d, q, cp, *names):
        for rp in names:
            wait(a_at(d, q, 1 - h, rp, cp), f"sa{d}{q}{rp}{cp}", cond_a(q))

    def l_get(d, q, rp):
        wait(l_at(d, q, rp), f"l{d}{q}{rp}", need(d))

    def l_fwd(d, q, rp, to, device):
        ref = l_at(d, q, rp)
        send(ref, ref, f"l{to}{rp}", device, need(d))

    def a_own(cp, ways):
        src = cut(a_ref, 0, "", cp)
        for role, device, cond in ways:
            send(src, a_at(0, 0, h, "", cp), f"a{role}{cp}", device, cond)

    def l_own(rp, ways):
        src = cut(l_ref, 0, rp, "")
        for role, device in ways:
            send(src, l_at(0, 0, rp), f"l{role}{rp}", device, need(0))

    def left_stage(stage, rp, cp):
        lo, n = row_part[rp]
        at, m = col_part[cp]
        at_rows, at_cols = pl.ds(lo, n), pl.ds(at, m)

        def stage_of(d, q, first):
            return jnp.where((q == 0) | (d == 0), first, first + 1)

        def step(k, carry):
            sa = stage_of((k % 4 - x + 4) % 4, (k // 4 + zl) % 2, 1 if cp == "L" else 3)
            sl = stage_of((k // 2 - y + 4) % 4, (k % 2 + zh) % 2, 1 if rp == "t" else 3)

            @pl.when((jnp.maximum(sa, sl) == stage) & (k <= p))
            def _():
                krow = pl.multiple_of(k * cols, cols)
                acc[at_rows, at_cols] += jnp.dot(
                    lbuf[k, at_rows], abuf[pl.ds(krow, cols), at_cols],
                    preferred_element_type=F32)

            return carry

        lax.fori_loop(0, 8, step, 0)

    def f_at(d, q, hh, rp, cp):
        return cut(fbuf.at[kap(x + d, zl + q, hh)], hh * rows, rp, cp)

    def finish(rp, cp):
        lo, n = row_part[rp]
        at, m = col_part[cp]
        lbf[pl.ds(lo, n), pl.ds(at, m)] = acc[pl.ds(lo, n), pl.ds(at, m)].astype(BF16)
        src = cut(lbf, 0, rp, cp)
        dst = cut(fbuf.at[c], h * rows, rp, cp)
        i = send_n[0]
        send_n[0] += 1
        landed = rsem.at[rid(f"f00{rp}{cp}")]
        copy = pltpu.make_async_remote_copy(
            src, dst, ssem.at[i], landed, device_id=t_dst,
            device_id_type=pl.DeviceIdType.MESH)
        when(jnp.logical_not(t_self), copy.start)
        when(t_self, lambda: pltpu.make_async_copy(src, dst, landed).start())
        sends.append((jnp.logical_not(t_self), copy))

    def f_fwd(d, q, piece, to, device):
        ref = f_at(d, q, h, *piece)
        send(ref, ref, "f" + to + piece, device)

    def f_get(piece, *roles):
        for d, q in roles:
            ref = f_at(d, q, h, *piece)
            wait(ref, f"f{d}{q}{piece}")
            if (d, q) == (0, 0):
                f_fwd(d, q, piece, "30", xp)
                f_fwd(d, q, piece, "10", xm)
                f_fwd(d, q, piece, "01", zp)
            elif (d, q) == (3, 0) and piece in ("tL", "bR"):
                f_fwd(d, q, piece, "20", xp)
            elif (d, q) == (1, 0) and piece in ("tR", "bL"):
                f_fwd(d, q, piece, "20", xm)
            elif (d, q) == (0, 1):
                f_fwd(d, q, piece, "31", xp)
                f_fwd(d, q, piece, "11", xm)
            elif (d, q) == (2, 0):
                f_fwd(d, q, piece, "21", zp)
            send(ref, ref, f"sf{d}{q}{piece}", sib)

    def out_stage(piece, *roles):
        for d, q in roles:
            wait(f_at(d, q, 1 - h, *piece), f"sf{d}{q}{piece}")
        (lo, n), at_cols = row_part[piece[0]], pl.ds(*col_part[piece[1]])

        def pick(j, values):
            v = values[0]
            for i, value in enumerate(values[1:], 1):
                v = jnp.where(j == i, value, v)
            return v

        def step(i, carry):
            j, hh = i // 2, i % 2
            d, q = pick(j, [r[0] for r in roles]), pick(j, [r[1] for r in roles])
            k = kap(x + d, zl + q, hh)

            @pl.when(k <= p)
            def _():
                at = pl.ds(pl.multiple_of(hh * rows + lo, 32), n)
                o_ref[at, :] += lax.dot_general(
                    fbuf[k, at, at_cols], lbuf[k, :, at_cols], (((1,), (1,)), ((), ())),
                    preferred_element_type=F32)
            return carry

        lax.fori_loop(0, 2 * len(roles), step, 0)

    ring = (("30", xp, None), ("10", xm, None))
    a_own("L", ring)
    l_own("t", (("30", yp), ("10", ym)))
    first = len(sends)
    a_own("L", (("01", zp, lower),))
    l_own("t", (("01", hp),))
    send(a_ref, a_at(0, 0, h, "", ""), "sa00", sib)
    ca = pltpu.make_async_copy(a_ref, a_at(0, 0, h, "", ""), csem.at[0])
    cl = pltpu.make_async_copy(l_ref, l_at(0, 0, ""), csem.at[1])
    ca.start()
    cl.start()
    acc[...] = jnp.zeros_like(acc)
    o_ref[...] = jnp.zeros_like(o_ref)
    ca.wait()
    cl.wait()

    l_get(3, 0, "t")
    l_fwd(3, 0, "t0", "20", yp)
    l_get(1, 0, "t")
    l_fwd(1, 0, "t1", "20", ym)
    l_own("b", (("30", yp), ("10", ym)))
    a_get(3, 0, "", "L")
    a_fwd(3, 0, "u", "L", "20", xp, None)
    a_get(1, 0, "", "L")
    a_fwd(1, 0, "v", "L", "20", xm, None)
    a_own("R", ring)
    for cond, copy in sends[first:first + 2]:
        when(cond, copy.wait_send)
    del sends[first:first + 2]
    a_own("R", (("01", zp, lower),))
    l_own("b", (("01", hp),))
    l_get(0, 1, "t")
    l_fwd(0, 1, "t", "31", yp)
    l_fwd(0, 1, "t", "11", ym)
    a_get(0, 1, "", "L")
    a_fwd(0, 1, "", "L", "31", xp, upper)
    a_fwd(0, 1, "", "L", "11", xm, upper)
    a_get(2, 0, "u", "L")
    a_get(2, 0, "v", "L")
    l_get(3, 0, "b")
    l_fwd(3, 0, "b0", "20", yp)
    l_get(1, 0, "b")
    l_fwd(1, 0, "b1", "20", ym)
    a_get(3, 0, "", "R")
    a_fwd(3, 0, "u", "R", "20", xp, None)
    a_get(1, 0, "", "R")
    a_fwd(1, 0, "v", "R", "20", xm, None)
    l_get(2, 0, "t0")
    l_get(2, 0, "t1")
    wait(a_at(0, 0, 1 - h, "", ""), "sa00")
    for d in (3, 1):
        a_sib(d, 0, "L", "")
    a_sib(0, 1, "L", "")
    a_sib(2, 0, "L", "u", "v")
    left_stage(1, "t", "L")

    l_get(3, 1, "t")
    l_fwd(3, 1, "t0", "21", yp)
    l_get(1, 1, "t")
    l_fwd(1, 1, "t1", "21", ym)
    a_get(3, 1, "", "L")
    a_fwd(3, 1, "u", "L", "21", xp, upper)
    a_get(1, 1, "", "L")
    a_fwd(1, 1, "v", "L", "21", xm, upper)
    l_get(0, 1, "b")
    l_fwd(0, 1, "b", "31", yp)
    l_fwd(0, 1, "b", "11", ym)
    a_get(0, 1, "", "R")
    a_fwd(0, 1, "", "R", "31", xp, upper)
    a_fwd(0, 1, "", "R", "11", xm, upper)
    a_get(2, 0, "u", "R")
    a_get(2, 0, "v", "R")
    for rp in "uv":
        a_get(2, 1, rp, "L")
    l_get(2, 1, "t0")
    l_get(2, 1, "t1")
    for d in (3, 1):
        a_sib(d, 1, "L", "")
    a_sib(2, 1, "L", "u", "v")
    left_stage(2, "t", "L")
    finish("t", "L")

    l_get(2, 0, "b0")
    l_get(2, 0, "b1")
    for d in (3, 1):
        a_sib(d, 0, "R", "")
    a_sib(0, 1, "R", "")
    a_sib(2, 0, "R", "u", "v")
    left_stage(3, "b", "L")
    left_stage(3, "t", "R")
    left_stage(3, "b", "R")

    a_get(3, 1, "", "R")
    a_fwd(3, 1, "u", "R", "21", xp, upper)
    a_get(1, 1, "", "R")
    a_fwd(1, 1, "v", "R", "21", xm, upper)
    l_get(3, 1, "b")
    l_fwd(3, 1, "b0", "21", yp)
    l_get(1, 1, "b")
    l_fwd(1, 1, "b1", "21", ym)
    f_get("tL", (0, 0))
    for rp in "uv":
        a_get(2, 1, rp, "R")
    for d in (3, 1):
        a_sib(d, 1, "R", "")
    a_sib(2, 1, "R", "u", "v")
    left_stage(4, "t", "R")
    finish("t", "R")
    l_get(2, 1, "b0")
    l_get(2, 1, "b1")
    left_stage(4, "b", "L")
    finish("b", "L")
    near = ((3, 0), (1, 0), (0, 1))
    far = ((3, 1), (1, 1), (2, 1))
    f_get("tL", *near)
    left_stage(4, "b", "R")
    finish("b", "R")

    order = (
        ("tR", 0, 0), ("bL", 0, 0), ("tL", 3, 1), ("tL", 1, 1), ("bR", 0, 0), ("tL", 2, 1),
        ("tR", 3, 0), ("tR", 1, 0), ("tR", 0, 1), ("bL", 3, 0), ("bL", 1, 0), ("bL", 0, 1),
        ("bR", 3, 0), ("bR", 1, 0), ("bR", 0, 1), ("tR", 2, 0), ("bL", 2, 0), ("bR", 2, 0),
        ("tR", 3, 1), ("tR", 1, 1), ("bL", 3, 1), ("bL", 1, 1), ("tR", 2, 1), ("bL", 2, 1),
        ("bR", 3, 1), ("bR", 1, 1), ("bR", 2, 1),
    )
    lag = 3
    f_get("tL", (2, 0))
    out_stage("tL", (0, 0), *near)
    out_stage("tL", (2, 0))
    for i, (piece, *role) in enumerate(order):
        f_get(piece, tuple(role))
        if i >= lag:
            piece, *role = order[i - lag]
            out_stage(piece, tuple(role))
    for piece, *role in order[len(order) - lag:]:
        out_stage(piece, tuple(role))
    drain()


SENDS, RECVS = 200, 200


def body(matrix, inverse_factor):
    rows, cols = matrix.shape
    order = 16 * rows
    return pl.pallas_call(
        kernel,
        out_shape=jax.ShapeDtypeStruct((cols, rows), F32),
        in_specs=[pl.BlockSpec(memory_space=pl.ANY)] * 2,
        out_specs=pl.BlockSpec(memory_space=pltpu.VMEM),
        scratch_shapes=[
            pltpu.VMEM((order, cols), BF16),
            pltpu.VMEM((8, rows, cols), BF16),
            pltpu.VMEM((8, cols, cols), BF16),
            pltpu.VMEM((rows, cols), F32),
            pltpu.VMEM((rows, cols), BF16),
            pltpu.SemaphoreType.DMA((SENDS,)),
            pltpu.SemaphoreType.DMA((RECVS,)),
            pltpu.SemaphoreType.DMA((2,)),
        ],
        compiler_params=pltpu.CompilerParams(
            collective_id=0, has_side_effects=True, vmem_limit_bytes=63 * 1024 * 1024),
        cost_estimate=pl.CostEstimate(
            flops=4 * rows * cols * order, bytes_accessed=8 * rows * cols, transcendentals=0),
    )(matrix, inverse_factor)


def solution(mesh):
    in_specs = (P("row", "col"), P("row", "col"))
    return jax.shard_map(body, mesh=mesh, in_specs=in_specs, out_specs=P("col", "row"), check_vma=False)
```

```python
import jax
import jax.numpy as jnp
from jax import lax
from jax.experimental import pallas as pl
from jax.experimental.pallas import tpu as pltpu
from jax.sharding import PartitionSpec as P

BF16, F32 = jnp.bfloat16, jnp.float32


def kernel(a_ref, l_ref, o_ref, abuf, lbuf, fbuf, acc, lbf, ssem, rsem, csem):
    rows, cols = a_ref.shape
    row, c = lax.axis_index("row"), lax.axis_index("col")
    h, p = row % 2, row // 2
    x, zl = p % 4, p // 4
    y, zh = c // 2, c % 2

    def chip(px, pz):
        return (pz % 2) * 4 + px % 4

    def on_row(pp):
        return (pp * 2 + h, c)

    xp, xm = on_row(chip(x + 1, zl)), on_row(chip(x + 3, zl))
    zp = on_row(chip(x, zl + 1))
    sib = (p * 2 + 1 - h, c)
    yp = (row, ((y + 1) % 4) * 2 + zh)
    ym = (row, ((y + 3) % 4) * 2 + zh)
    hp = (row, y * 2 + 1 - zh)

    t_chip = chip(x + y + 2 * h, zh + h)
    t_dst = (t_chip * 2 + h, p)

    def kap(px, pz, hh):
        return 2 * ((px - c % 4 - 2 * hh + 8) % 4) + (pz + hh) % 2

    t_src = (c * 2 + h, kap(x, zl, h))
    t_self = (p == c) & (t_chip == p)

    half = rows // 2
    send_n = [0]
    recv_ids = {}
    sends = []

    def when(cond, f):
        if cond is None:
            f()
        else:
            pl.when(cond)(f)

    def rid(role):
        return recv_ids.setdefault(role, len(recv_ids))

    def send(src, dst, role, device, cond=None):
        i = send_n[0]
        send_n[0] += 1
        cp = pltpu.make_async_remote_copy(
            src, dst, ssem.at[i], rsem.at[rid(role)], device_id=device,
            device_id_type=pl.DeviceIdType.MESH)
        when(cond, cp.start)
        sends.append((cond, cp))

    def drain():
        for cond, cp in sends:
            when(cond, cp.wait_send)
        sends.clear()

    def wait(ref, role, cond=None):
        cp = pltpu.make_async_remote_copy(
            ref, ref, ssem.at[0], rsem.at[rid(role)], device_id=xp,
            device_id_type=pl.DeviceIdType.MESH)
        when(cond, cp.wait_recv)

    barrier = pltpu.get_barrier_semaphore()
    for device in (xp, xm, zp, sib, yp, ym, hp):
        pl.semaphore_signal(barrier, inc=1, device_id=device, device_id_type=pl.DeviceIdType.MESH)

    @pl.when(jnp.logical_not(t_self))
    def _():
        for device in (t_dst, t_src):
            pl.semaphore_signal(barrier, inc=1, device_id=device, device_id_type=pl.DeviceIdType.MESH)

    pl.semaphore_wait(barrier, jnp.where(t_self, 7, 9))

    top, split = half, (cols // 256 + 1) * 128

    def halves(name, lo, n):
        return {name: (lo, n), name + "0": (lo, n // 2), name + "1": (lo + n // 2, n // 2)}

    row_part = {"": (0, rows), "u": (0, half), "v": (half, half),
                **halves("t", 0, top), **halves("b", top, rows - top)}
    col_part = {"": (0, cols), "L": (0, split), "R": (split, cols - split)}
    upper, lower = zl == 1, zl == 0

    def cut(ref, start, rp, cp):
        lo, n = row_part[rp]
        at, m = col_part[cp]
        return ref.at[pl.ds(pl.multiple_of(start + lo, 16), n), pl.ds(at, m)]

    def need(d):
        return upper | ((y + d) % 4 <= 1)

    def a_at(d, q, hh, rp, cp):
        return cut(abuf, (chip(x + d, zl + q) * 2 + hh) * rows, rp, cp)

    def l_at(d, q, rp):
        return cut(lbuf.at[((y + d) % 4) * 2 + (zh + q) % 2], 0, rp, "")

    def cond_a(q):
        return upper if q else None

    def a_get(d, q, rp, cp):
        ref = a_at(d, q, h, rp, cp)
        wait(ref, f"a{d}{q}{rp}{cp}", cond_a(q))
        send(ref, ref, f"sa{d}{q}{rp}{cp}", sib, cond_a(q))

    def a_fwd(d, q, rp, cp, to, device, cond):
        ref = a_at(d, q, h, rp, cp)
        send(ref, ref, f"a{to}{rp}{cp}", device, cond)

    def a_sib(d, q, cp, *names):
        for rp in names:
            wait(a_at(d, q, 1 - h, rp, cp), f"sa{d}{q}{rp}{cp}", cond_a(q))

    def l_get(d, q, rp):
        wait(l_at(d, q, rp), f"l{d}{q}{rp}", need(d))

    def l_fwd(d, q, rp, to, device):
        ref = l_at(d, q, rp)
        send(ref, ref, f"l{to}{rp}", device, need(d))

    def a_own(cp, ways):
        src = cut(a_ref, 0, "", cp)
        for role, device, cond in ways:
            send(src, a_at(0, 0, h, "", cp), f"a{role}{cp}", device, cond)

    def l_own(rp, ways):
        src = cut(l_ref, 0, rp, "")
        for role, device in ways:
            send(src, l_at(0, 0, rp), f"l{role}{rp}", device, need(0))

    def left_stage(stage, rp, cp):
        lo, n = row_part[rp]
        at, m = col_part[cp]
        at_rows, at_cols = pl.ds(lo, n), pl.ds(at, m)

        def stage_of(d, q, first):
            return jnp.where((q == 0) | (d == 0), first, first + 1)

        def step(k, carry):
            sa = stage_of((k % 4 - x + 4) % 4, (k // 4 + zl) % 2, 1 if cp == "L" else 3)
            sl = stage_of((k // 2 - y + 4) % 4, (k % 2 + zh) % 2, 1 if rp == "t" else 3)

            @pl.when((jnp.maximum(sa, sl) == stage) & (k <= p))
            def _():
                krow = pl.multiple_of(k * cols, cols)
                acc[at_rows, at_cols] += jnp.dot(
                    lbuf[k, at_rows], abuf[pl.ds(krow, cols), at_cols],
                    preferred_element_type=F32)

            return carry

        lax.fori_loop(0, 8, step, 0)

    def f_at(d, q, hh, rp, cp):
        return cut(fbuf.at[kap(x + d, zl + q, hh)], hh * rows, rp, cp)

    def finish(rp, cp):
        lo, n = row_part[rp]
        at, m = col_part[cp]
        lbf[pl.ds(lo, n), pl.ds(at, m)] = acc[pl.ds(lo, n), pl.ds(at, m)].astype(BF16)
        src = cut(lbf, 0, rp, cp)
        dst = cut(fbuf.at[c], h * rows, rp, cp)
        i = send_n[0]
        send_n[0] += 1
        landed = rsem.at[rid(f"f00{rp}{cp}")]
        copy = pltpu.make_async_remote_copy(
            src, dst, ssem.at[i], landed, device_id=t_dst,
            device_id_type=pl.DeviceIdType.MESH)
        when(jnp.logical_not(t_self), copy.start)
        when(t_self, lambda: pltpu.make_async_copy(src, dst, landed).start())
        sends.append((jnp.logical_not(t_self), copy))

    def f_need(d, q, hh, who):
        return who | (kap(x + d, zl + q, hh) < 4)

    def f_fwd(d, q, piece, to, device):
        ref = f_at(d, q, h, *piece)
        cond = None
        if to[1] == "1":
            cond = f_need(d, q, h, upper if q else lower)
        send(ref, ref, "f" + to + piece, device, cond)

    def f_get(piece, *roles):
        for d, q in roles:
            ref = f_at(d, q, h, *piece)
            cond = f_need(d, q, h, upper) if q else None
            wait(ref, f"f{d}{q}{piece}", cond)
            if (d, q) == (0, 0):
                f_fwd(d, q, piece, "30", xp)
                f_fwd(d, q, piece, "10", xm)
                f_fwd(d, q, piece, "01", zp)
            elif (d, q) == (3, 0) and piece in ("tL", "bR"):
                f_fwd(d, q, piece, "20", xp)
            elif (d, q) == (1, 0) and piece in ("tR", "bL"):
                f_fwd(d, q, piece, "20", xm)
            elif (d, q) == (0, 1):
                f_fwd(d, q, piece, "31", xp)
                f_fwd(d, q, piece, "11", xm)
            elif (d, q) == (2, 0):
                f_fwd(d, q, piece, "21", zp)
            send(ref, ref, f"sf{d}{q}{piece}", sib, cond)

    def out_stage(piece, *roles):
        for d, q in roles:
            cond = f_need(d, q, 1 - h, upper) if q else None
            wait(f_at(d, q, 1 - h, *piece), f"sf{d}{q}{piece}", cond)
        (lo, n), at_cols = row_part[piece[0]], pl.ds(*col_part[piece[1]])

        def pick(j, values):
            v = values[0]
            for i, value in enumerate(values[1:], 1):
                v = jnp.where(j == i, value, v)
            return v

        def step(i, carry):
            j, hh = i // 2, i % 2
            d, q = pick(j, [r[0] for r in roles]), pick(j, [r[1] for r in roles])
            k = kap(x + d, zl + q, hh)

            @pl.when(k <= p)
            def _():
                at = pl.ds(pl.multiple_of(hh * rows + lo, 32), n)
                o_ref[at, :] += lax.dot_general(
                    fbuf[k, at, at_cols], lbuf[k, :, at_cols], (((1,), (1,)), ((), ())),
                    preferred_element_type=F32)
            return carry

        lax.fori_loop(0, 2 * len(roles), step, 0)

    ring = (("30", xp, None), ("10", xm, None))
    first = len(sends)
    l_own("t", (("01", hp),))
    a_own("L", (("01", zp, lower),))
    a_own("L", ring)
    l_own("t", (("30", yp), ("10", ym)))
    send(a_ref, a_at(0, 0, h, "", ""), "sa00", sib)
    ca = pltpu.make_async_copy(a_ref, a_at(0, 0, h, "", ""), csem.at[0])
    cl = pltpu.make_async_copy(l_ref, l_at(0, 0, ""), csem.at[1])
    ca.start()
    cl.start()
    acc[...] = jnp.zeros_like(acc)
    o_ref[...] = jnp.zeros_like(o_ref)
    ca.wait()
    cl.wait()

    l_get(3, 0, "t")
    l_fwd(3, 0, "t0", "20", yp)
    l_get(1, 0, "t")
    l_fwd(1, 0, "t1", "20", ym)
    l_own("b", (("30", yp), ("10", ym)))
    a_get(3, 0, "", "L")
    a_fwd(3, 0, "u", "L", "20", xp, None)
    a_get(1, 0, "", "L")
    a_fwd(1, 0, "v", "L", "20", xm, None)
    a_own("R", ring)
    for cond, copy in sends[first:first + 2]:
        when(cond, copy.wait_send)
    del sends[first:first + 2]
    a_own("R", (("01", zp, lower),))
    l_own("b", (("01", hp),))
    l_get(0, 1, "t")
    l_fwd(0, 1, "t", "31", yp)
    l_fwd(0, 1, "t", "11", ym)
    a_get(0, 1, "", "L")
    a_fwd(0, 1, "", "L", "31", xp, upper)
    a_fwd(0, 1, "", "L", "11", xm, upper)
    a_get(2, 0, "u", "L")
    a_get(2, 0, "v", "L")
    l_get(3, 0, "b")
    l_fwd(3, 0, "b0", "20", yp)
    l_get(1, 0, "b")
    l_fwd(1, 0, "b1", "20", ym)
    a_get(3, 0, "", "R")
    a_fwd(3, 0, "u", "R", "20", xp, None)
    a_get(1, 0, "", "R")
    a_fwd(1, 0, "v", "R", "20", xm, None)
    l_get(2, 0, "t0")
    l_get(2, 0, "t1")
    wait(a_at(0, 0, 1 - h, "", ""), "sa00")
    for d in (3, 1):
        a_sib(d, 0, "L", "")
    a_sib(0, 1, "L", "")
    a_sib(2, 0, "L", "u", "v")
    left_stage(1, "t", "L")

    l_get(3, 1, "t")
    l_fwd(3, 1, "t0", "21", yp)
    l_get(1, 1, "t")
    l_fwd(1, 1, "t1", "21", ym)
    a_get(3, 1, "", "L")
    a_fwd(3, 1, "u", "L", "21", xp, upper)
    a_get(1, 1, "", "L")
    a_fwd(1, 1, "v", "L", "21", xm, upper)
    l_get(0, 1, "b")
    l_fwd(0, 1, "b", "31", yp)
    l_fwd(0, 1, "b", "11", ym)
    a_get(0, 1, "", "R")
    a_fwd(0, 1, "", "R", "31", xp, upper)
    a_fwd(0, 1, "", "R", "11", xm, upper)
    a_get(2, 0, "u", "R")
    a_get(2, 0, "v", "R")
    for rp in "uv":
        a_get(2, 1, rp, "L")
    l_get(2, 1, "t0")
    l_get(2, 1, "t1")
    for d in (3, 1):
        a_sib(d, 1, "L", "")
    a_sib(2, 1, "L", "u", "v")
    left_stage(2, "t", "L")
    finish("t", "L")

    l_get(2, 0, "b0")
    l_get(2, 0, "b1")
    for d in (3, 1):
        a_sib(d, 0, "R", "")
    a_sib(0, 1, "R", "")
    a_sib(2, 0, "R", "u", "v")
    left_stage(3, "b", "L")
    left_stage(3, "t", "R")
    left_stage(3, "b", "R")

    a_get(3, 1, "", "R")
    a_fwd(3, 1, "u", "R", "21", xp, upper)
    a_get(1, 1, "", "R")
    a_fwd(1, 1, "v", "R", "21", xm, upper)
    l_get(3, 1, "b")
    l_fwd(3, 1, "b0", "21", yp)
    l_get(1, 1, "b")
    l_fwd(1, 1, "b1", "21", ym)
    f_get("tL", (0, 0))
    for rp in "uv":
        a_get(2, 1, rp, "R")
    for d in (3, 1):
        a_sib(d, 1, "R", "")
    a_sib(2, 1, "R", "u", "v")
    left_stage(4, "t", "R")
    finish("t", "R")
    l_get(2, 1, "b0")
    l_get(2, 1, "b1")
    left_stage(4, "b", "L")
    finish("b", "L")
    near = ((3, 0), (1, 0), (0, 1))
    far = ((3, 1), (1, 1), (2, 1))
    f_get("tL", *near)
    left_stage(4, "b", "R")
    finish("b", "R")

    order = (
        ("tR", 0, 0), ("bL", 0, 0), ("tL", 3, 1), ("tL", 1, 1), ("bR", 0, 0), ("tL", 2, 1),
        ("tR", 3, 0), ("tR", 1, 0), ("tR", 0, 1), ("bL", 3, 0), ("bL", 1, 0), ("bL", 0, 1),
        ("bR", 3, 0), ("bR", 1, 0), ("bR", 0, 1), ("tR", 2, 0), ("bL", 2, 0), ("bR", 2, 0),
        ("tR", 3, 1), ("tR", 1, 1), ("bL", 3, 1), ("bL", 1, 1), ("tR", 2, 1), ("bL", 2, 1),
        ("bR", 3, 1), ("bR", 1, 1), ("bR", 2, 1),
    )
    lag = 2
    f_get("tL", (2, 0))
    out_stage("tL", (0, 0), *near)
    out_stage("tL", (2, 0))
    for i, (piece, *role) in enumerate(order):
        f_get(piece, tuple(role))
        if i >= lag:
            piece, *role = order[i - lag]
            out_stage(piece, tuple(role))
    for piece, *role in order[len(order) - lag:]:
        out_stage(piece, tuple(role))
    drain()


SENDS, RECVS = 200, 200


def body(matrix, inverse_factor):
    rows, cols = matrix.shape
    order = 16 * rows
    return pl.pallas_call(
        kernel,
        out_shape=jax.ShapeDtypeStruct((cols, rows), F32),
        in_specs=[pl.BlockSpec(memory_space=pl.ANY)] * 2,
        out_specs=pl.BlockSpec(memory_space=pltpu.VMEM),
        scratch_shapes=[
            pltpu.VMEM((order, cols), BF16),
            pltpu.VMEM((8, rows, cols), BF16),
            pltpu.VMEM((8, cols, cols), BF16),
            pltpu.VMEM((rows, cols), F32),
            pltpu.VMEM((rows, cols), BF16),
            pltpu.SemaphoreType.DMA((SENDS,)),
            pltpu.SemaphoreType.DMA((RECVS,)),
            pltpu.SemaphoreType.DMA((2,)),
        ],
        compiler_params=pltpu.CompilerParams(
            collective_id=0, has_side_effects=True, vmem_limit_bytes=63 * 1024 * 1024),
        cost_estimate=pl.CostEstimate(
            flops=4 * rows * cols * order, bytes_accessed=8 * rows * cols, transcendentals=0),
    )(matrix, inverse_factor)


def solution(mesh):
    in_specs = (P("row", "col"), P("row", "col"))
    return jax.shard_map(body, mesh=mesh, in_specs=in_specs, out_specs=P("col", "row"), check_vma=False)
```

```python
import jax
import jax.numpy as jnp
from jax import lax
from jax.experimental import pallas as pl
from jax.experimental.pallas import tpu as pltpu
from jax.sharding import PartitionSpec as P

BF16, F32 = jnp.bfloat16, jnp.float32


def kernel(a_ref, l_ref, o_ref, abuf, lbuf, fbuf, acc, lbf, ssem, rsem, csem):
    rows, cols = a_ref.shape
    row, c = lax.axis_index("row"), lax.axis_index("col")
    h, p = row % 2, row // 2
    x, zl = p % 4, p // 4
    y, zh = c // 2, c % 2

    def chip(px, pz):
        return (pz % 2) * 4 + px % 4

    def on_row(pp):
        return (pp * 2 + h, c)

    xp, xm = on_row(chip(x + 1, zl)), on_row(chip(x + 3, zl))
    zp = on_row(chip(x, zl + 1))
    sib = (p * 2 + 1 - h, c)
    yp = (row, ((y + 1) % 4) * 2 + zh)
    ym = (row, ((y + 3) % 4) * 2 + zh)
    hp = (row, y * 2 + 1 - zh)

    t_chip = chip(x + y + 2 * h, zh + h)
    t_dst = (t_chip * 2 + h, p)

    def kap(px, pz, hh):
        return 2 * ((px - c % 4 - 2 * hh + 8) % 4) + (pz + hh) % 2

    t_src = (c * 2 + h, kap(x, zl, h))
    t_self = (p == c) & (t_chip == p)

    half = rows // 2
    send_n = [0]
    recv_ids = {}
    sends = []

    def when(cond, f):
        if cond is None:
            f()
        else:
            pl.when(cond)(f)

    def rid(role):
        return recv_ids.setdefault(role, len(recv_ids))

    def send(src, dst, role, device, cond=None):
        i = send_n[0]
        send_n[0] += 1
        cp = pltpu.make_async_remote_copy(
            src, dst, ssem.at[i], rsem.at[rid(role)], device_id=device,
            device_id_type=pl.DeviceIdType.MESH)
        when(cond, cp.start)
        sends.append((cond, cp))

    def drain():
        for cond, cp in sends:
            when(cond, cp.wait_send)
        sends.clear()

    def wait(ref, role, cond=None):
        cp = pltpu.make_async_remote_copy(
            ref, ref, ssem.at[0], rsem.at[rid(role)], device_id=xp,
            device_id_type=pl.DeviceIdType.MESH)
        when(cond, cp.wait_recv)

    barrier = pltpu.get_barrier_semaphore()
    for device in (xp, xm, zp, sib, yp, ym, hp):
        pl.semaphore_signal(barrier, inc=1, device_id=device, device_id_type=pl.DeviceIdType.MESH)

    @pl.when(jnp.logical_not(t_self))
    def _():
        for device in (t_dst, t_src):
            pl.semaphore_signal(barrier, inc=1, device_id=device, device_id_type=pl.DeviceIdType.MESH)

    pl.semaphore_wait(barrier, jnp.where(t_self, 7, 9))

    top, split = half, (cols // 256 + 1) * 128

    def halves(name, lo, n):
        return {name: (lo, n), name + "0": (lo, n // 2), name + "1": (lo + n // 2, n // 2)}

    row_part = {"": (0, rows), "u": (0, half), "v": (half, half),
                **halves("t", 0, top), **halves("b", top, rows - top)}
    col_part = {"": (0, cols), "L": (0, split), "R": (split, cols - split)}
    upper, lower = zl == 1, zl == 0

    def cut(ref, start, rp, cp):
        lo, n = row_part[rp]
        at, m = col_part[cp]
        return ref.at[pl.ds(pl.multiple_of(start + lo, 16), n), pl.ds(at, m)]

    def need(d):
        return upper | ((y + d) % 4 <= 1)

    def a_at(d, q, hh, rp, cp):
        return cut(abuf, (chip(x + d, zl + q) * 2 + hh) * rows, rp, cp)

    def l_at(d, q, rp):
        return cut(lbuf.at[((y + d) % 4) * 2 + (zh + q) % 2], 0, rp, "")

    def cond_a(q):
        return upper if q else None

    def a_get(d, q, rp, cp):
        ref = a_at(d, q, h, rp, cp)
        wait(ref, f"a{d}{q}{rp}{cp}", cond_a(q))
        send(ref, ref, f"sa{d}{q}{rp}{cp}", sib, cond_a(q))

    def a_fwd(d, q, rp, cp, to, device, cond):
        ref = a_at(d, q, h, rp, cp)
        send(ref, ref, f"a{to}{rp}{cp}", device, cond)

    def a_sib(d, q, cp, *names):
        for rp in names:
            wait(a_at(d, q, 1 - h, rp, cp), f"sa{d}{q}{rp}{cp}", cond_a(q))

    def l_get(d, q, rp):
        wait(l_at(d, q, rp), f"l{d}{q}{rp}", need(d))

    def l_fwd(d, q, rp, to, device):
        ref = l_at(d, q, rp)
        send(ref, ref, f"l{to}{rp}", device, need(d))

    def a_own(cp, ways):
        src = cut(a_ref, 0, "", cp)
        for role, device, cond in ways:
            send(src, a_at(0, 0, h, "", cp), f"a{role}{cp}", device, cond)

    def l_own(rp, ways):
        src = cut(l_ref, 0, rp, "")
        for role, device in ways:
            send(src, l_at(0, 0, rp), f"l{role}{rp}", device, need(0))

    def left_stage(stage, rp, cp):
        lo, n = row_part[rp]
        at, m = col_part[cp]
        at_rows, at_cols = pl.ds(lo, n), pl.ds(at, m)

        def stage_of(d, q, first):
            return jnp.where((q == 0) | (d == 0), first, first + 1)

        def step(k, carry):
            sa = stage_of((k % 4 - x + 4) % 4, (k // 4 + zl) % 2, 1 if cp == "L" else 3)
            sl = stage_of((k // 2 - y + 4) % 4, (k % 2 + zh) % 2, 1 if rp == "t" else 3)

            @pl.when((jnp.maximum(sa, sl) == stage) & (k <= p))
            def _():
                krow = pl.multiple_of(k * cols, cols)
                acc[at_rows, at_cols] += jnp.dot(
                    lbuf[k, at_rows], abuf[pl.ds(krow, cols), at_cols],
                    preferred_element_type=F32)

            return carry

        lax.fori_loop(0, 8, step, 0)

    def f_at(d, q, hh, rp, cp):
        return cut(fbuf.at[kap(x + d, zl + q, hh)], hh * rows, rp, cp)

    def finish(rp, cp):
        lo, n = row_part[rp]
        at, m = col_part[cp]
        lbf[pl.ds(lo, n), pl.ds(at, m)] = acc[pl.ds(lo, n), pl.ds(at, m)].astype(BF16)
        src = cut(lbf, 0, rp, cp)
        dst = cut(fbuf.at[c], h * rows, rp, cp)
        i = send_n[0]
        send_n[0] += 1
        landed = rsem.at[rid(f"f00{rp}{cp}")]
        copy = pltpu.make_async_remote_copy(
            src, dst, ssem.at[i], landed, device_id=t_dst,
            device_id_type=pl.DeviceIdType.MESH)
        when(jnp.logical_not(t_self), copy.start)
        when(t_self, lambda: pltpu.make_async_copy(src, dst, landed).start())
        sends.append((jnp.logical_not(t_self), copy))

    def f_need(d, q, hh, who):
        return who | (kap(x + d, zl + q, hh) < 4)

    def f_fwd(d, q, piece, to, device):
        ref = f_at(d, q, h, *piece)
        cond = None
        if to[1] == "1":
            cond = f_need(d, q, h, upper if q else lower)
        send(ref, ref, "f" + to + piece, device, cond)

    def f_get(piece, *roles):
        for d, q in roles:
            ref = f_at(d, q, h, *piece)
            cond = f_need(d, q, h, upper) if q else None
            wait(ref, f"f{d}{q}{piece}", cond)
            if (d, q) == (0, 0):
                f_fwd(d, q, piece, "30", xp)
                f_fwd(d, q, piece, "10", xm)
                f_fwd(d, q, piece, "01", zp)
            elif (d, q) == (3, 0) and piece in ("tL", "bR"):
                f_fwd(d, q, piece, "20", xp)
            elif (d, q) == (1, 0) and piece in ("tR", "bL"):
                f_fwd(d, q, piece, "20", xm)
            elif (d, q) == (0, 1):
                f_fwd(d, q, piece, "31", xp)
                f_fwd(d, q, piece, "11", xm)
            elif (d, q) == (2, 0):
                f_fwd(d, q, piece, "21", zp)
            send(ref, ref, f"sf{d}{q}{piece}", sib, cond)

    def out_stage(piece, *roles):
        for d, q in roles:
            cond = f_need(d, q, 1 - h, upper) if q else None
            wait(f_at(d, q, 1 - h, *piece), f"sf{d}{q}{piece}", cond)
        (lo, n), at_cols = row_part[piece[0]], pl.ds(*col_part[piece[1]])

        def pick(j, values):
            v = values[0]
            for i, value in enumerate(values[1:], 1):
                v = jnp.where(j == i, value, v)
            return v

        def step(i, carry):
            j, hh = i // 2, i % 2
            d, q = pick(j, [r[0] for r in roles]), pick(j, [r[1] for r in roles])
            k = kap(x + d, zl + q, hh)

            @pl.when(k <= p)
            def _():
                at = pl.ds(pl.multiple_of(hh * rows + lo, 32), n)
                o_ref[at, :] += lax.dot_general(
                    fbuf[k, at, at_cols], lbuf[k, :, at_cols], (((1,), (1,)), ((), ())),
                    preferred_element_type=F32)
            return carry

        lax.fori_loop(0, 2 * len(roles), step, 0)

    ring = (("30", xp, None), ("10", xm, None))
    first = len(sends)
    l_own("t", (("01", hp),))
    a_own("L", (("01", zp, lower),))
    a_own("L", ring)
    l_own("t", (("30", yp), ("10", ym)))
    send(a_ref, a_at(0, 0, h, "", ""), "sa00", sib)
    ca = pltpu.make_async_copy(a_ref, a_at(0, 0, h, "", ""), csem.at[0])
    cl = pltpu.make_async_copy(l_ref, l_at(0, 0, ""), csem.at[1])
    ca.start()
    cl.start()
    acc[...] = jnp.zeros_like(acc)
    o_ref[...] = jnp.zeros_like(o_ref)
    ca.wait()
    cl.wait()

    l_get(3, 0, "t")
    l_fwd(3, 0, "t0", "20", yp)
    l_get(1, 0, "t")
    l_fwd(1, 0, "t1", "20", ym)
    l_own("b", (("30", yp), ("10", ym)))
    a_get(3, 0, "", "L")
    a_fwd(3, 0, "u", "L", "20", xp, None)
    a_get(1, 0, "", "L")
    a_fwd(1, 0, "v", "L", "20", xm, None)
    a_own("R", ring)
    for cond, copy in sends[first:first + 2]:
        when(cond, copy.wait_send)
    del sends[first:first + 2]
    a_own("R", (("01", zp, lower),))
    l_own("b", (("01", hp),))
    l_get(0, 1, "t")
    l_fwd(0, 1, "t", "31", yp)
    l_fwd(0, 1, "t", "11", ym)
    a_get(0, 1, "", "L")
    a_fwd(0, 1, "", "L", "31", xp, upper)
    a_fwd(0, 1, "", "L", "11", xm, upper)
    a_get(2, 0, "u", "L")
    a_get(2, 0, "v", "L")
    l_get(3, 0, "b")
    l_fwd(3, 0, "b0", "20", yp)
    l_get(1, 0, "b")
    l_fwd(1, 0, "b1", "20", ym)
    a_get(3, 0, "", "R")
    a_fwd(3, 0, "u", "R", "20", xp, None)
    a_get(1, 0, "", "R")
    a_fwd(1, 0, "v", "R", "20", xm, None)
    l_get(2, 0, "t0")
    l_get(2, 0, "t1")
    wait(a_at(0, 0, 1 - h, "", ""), "sa00")
    for d in (3, 1):
        a_sib(d, 0, "L", "")
    a_sib(0, 1, "L", "")
    a_sib(2, 0, "L", "u", "v")
    left_stage(1, "t", "L")

    l_get(3, 1, "t")
    l_fwd(3, 1, "t0", "21", yp)
    l_get(1, 1, "t")
    l_fwd(1, 1, "t1", "21", ym)
    a_get(3, 1, "", "L")
    a_fwd(3, 1, "u", "L", "21", xp, upper)
    a_get(1, 1, "", "L")
    a_fwd(1, 1, "v", "L", "21", xm, upper)
    l_get(0, 1, "b")
    l_fwd(0, 1, "b", "31", yp)
    l_fwd(0, 1, "b", "11", ym)
    a_get(0, 1, "", "R")
    a_fwd(0, 1, "", "R", "31", xp, upper)
    a_fwd(0, 1, "", "R", "11", xm, upper)
    a_get(2, 0, "u", "R")
    a_get(2, 0, "v", "R")
    for rp in "uv":
        a_get(2, 1, rp, "L")
    l_get(2, 1, "t0")
    l_get(2, 1, "t1")
    for d in (3, 1):
        a_sib(d, 1, "L", "")
    a_sib(2, 1, "L", "u", "v")
    left_stage(2, "t", "L")
    finish("t", "L")

    l_get(2, 0, "b0")
    l_get(2, 0, "b1")
    for d in (3, 1):
        a_sib(d, 0, "R", "")
    a_sib(0, 1, "R", "")
    a_sib(2, 0, "R", "u", "v")
    left_stage(3, "b", "L")
    left_stage(3, "t", "R")
    left_stage(3, "b", "R")

    a_get(3, 1, "", "R")
    a_fwd(3, 1, "u", "R", "21", xp, upper)
    a_get(1, 1, "", "R")
    a_fwd(1, 1, "v", "R", "21", xm, upper)
    l_get(3, 1, "b")
    l_fwd(3, 1, "b0", "21", yp)
    l_get(1, 1, "b")
    l_fwd(1, 1, "b1", "21", ym)
    f_get("tL", (0, 0))
    for rp in "uv":
        a_get(2, 1, rp, "R")
    for d in (3, 1):
        a_sib(d, 1, "R", "")
    a_sib(2, 1, "R", "u", "v")
    left_stage(4, "t", "R")
    finish("t", "R")
    near = ((3, 0), (1, 0), (0, 1))
    f_get("tL", *near)
    l_get(2, 1, "b0")
    l_get(2, 1, "b1")
    left_stage(4, "b", "L")
    finish("b", "L")
    near = ((3, 0), (1, 0), (0, 1))
    far = ((3, 1), (1, 1), (2, 1))
    left_stage(4, "b", "R")
    finish("b", "R")

    order = (
        ("tR", 0, 0), ("bL", 0, 0), ("tL", 3, 1), ("tL", 1, 1), ("bR", 0, 0), ("tL", 2, 1),
        ("tR", 3, 0), ("tR", 1, 0), ("tR", 0, 1), ("bL", 3, 0), ("bL", 1, 0), ("bL", 0, 1),
        ("bR", 3, 0), ("bR", 1, 0), ("bR", 0, 1), ("tR", 2, 0), ("bL", 2, 0), ("bR", 2, 0),
        ("tR", 3, 1), ("tR", 1, 1), ("bL", 3, 1), ("bL", 1, 1), ("tR", 2, 1), ("bL", 2, 1),
        ("bR", 3, 1), ("bR", 1, 1), ("bR", 2, 1),
    )
    lag = 2
    f_get("tL", (2, 0))
    out_stage("tL", (0, 0), *near)
    out_stage("tL", (2, 0))
    for i, (piece, *role) in enumerate(order):
        f_get(piece, tuple(role))
        if i >= lag:
            piece, *role = order[i - lag]
            out_stage(piece, tuple(role))
    for piece, *role in order[len(order) - lag:]:
        out_stage(piece, tuple(role))
    drain()


SENDS, RECVS = 200, 200


def body(matrix, inverse_factor):
    rows, cols = matrix.shape
    order = 16 * rows
    return pl.pallas_call(
        kernel,
        out_shape=jax.ShapeDtypeStruct((cols, rows), F32),
        in_specs=[pl.BlockSpec(memory_space=pl.ANY)] * 2,
        out_specs=pl.BlockSpec(memory_space=pltpu.VMEM),
        scratch_shapes=[
            pltpu.VMEM((order, cols), BF16),
            pltpu.VMEM((8, rows, cols), BF16),
            pltpu.VMEM((8, cols, cols), BF16),
            pltpu.VMEM((rows, cols), F32),
            pltpu.VMEM((rows, cols), BF16),
            pltpu.SemaphoreType.DMA((SENDS,)),
            pltpu.SemaphoreType.DMA((RECVS,)),
            pltpu.SemaphoreType.DMA((2,)),
        ],
        compiler_params=pltpu.CompilerParams(
            collective_id=0, has_side_effects=True, vmem_limit_bytes=63 * 1024 * 1024),
        cost_estimate=pl.CostEstimate(
            flops=4 * rows * cols * order, bytes_accessed=8 * rows * cols, transcendentals=0),
    )(matrix, inverse_factor)


def solution(mesh):
    in_specs = (P("row", "col"), P("row", "col"))
    return jax.shard_map(body, mesh=mesh, in_specs=in_specs, out_specs=P("col", "row"), check_vma=False)
```
